32 devices in a mesh: group: 2 (over x), fsdp: 8 (over z, y), tp: 2 (over core).
Axes of the slice: x: 2, y: 2, z: 4, core: 2. Of those that a mesh axis runs over, the one named last changes fastest.
Arguments:
- tokens: bfloat16 [16384, 8192], P(('group', 'fsdp'), 'tp'), parts along dimension 0, may hold values from -6 to 6
- cotangent: bfloat16 [16384, 1024], P(('group', 'fsdp'), 'tp'), parts along dimension 0, may hold values from -0.059814453 to 0.059814453
- frozen_rows: bfloat16 [1024, 8192], P('fsdp', 'tp'), may hold values from -0.0625 to 0.0625
- rank_down: bfloat16 [1024, 8192], P(('group', 'fsdp'), 'tp'), parts along dimension 0, may hold values from -0.0625 to 0.0625
- rank_up: bfloat16 [1024, 1024], P(('group', 'fsdp'), 'tp'), parts along dimension 0, may hold values from -1.5 to 1.5
- counts: int32 [16], P(('group', 'fsdp')), parts along dimension 0, may hold values from 1 to 2, as said below
- tenants: int32 [32], P(('group', 'fsdp')), parts along dimension 0, may hold values from 0 to 31
Outputs:
- projected: bfloat16 [16384, 1024], P(('group', 'fsdp'), 'tp'), parts along dimension 0
- grad_down: float32 [1024, 8192], P(('group', 'fsdp'), 'tp'), parts along dimension 0
- grad_up: float32 [1024, 1024], P(('group', 'fsdp'), 'tp'), parts along dimension 0
The draws below stay inside these ranges and needn't reach their ends.
There are 2 independent parts, one for each index of `group`. The reference program is written for one: setup_inputs(seed, part) draws one part's arguments, and reference() takes and returns one part's arrays. A program takes and returns all parts, laid end to end along the dimension named above; an argument that names none is the same for every part. Nothing has to cross between parts.
Inputs may be any that keep to these rules, and one draw needn't show every extreme that they name: Device f holds counts[f] live blocks in its first slots; in every draw some device has all 2 slots live.
All inputs are finite; a program needn't handle non-finite values.
Results may differ from the reference program's by a relative error of at most 0.0045.
Values may be sent and summed in bfloat16 or wider, within the bound.
A program may use at most 128 MiB of HBM per device.

```python
import jax
import jax.numpy as jnp
from jax import lax

D = 8192
DV = 1024
RANK = 16
TENANTS = 32
BLOCK = 512
SLOTS = 2
TOKENS = 8192
N_FSDP = 8


def draw_counts(key, part):
    key = jax.random.fold_in(key, 11)
    base_key, heavy_key, top_key = jax.random.split(key, 3)
    base_counts = jax.random.randint(base_key, (N_FSDP,), 1, 3)
    heavy_pick = jax.random.randint(heavy_key, (N_FSDP,), 0, 4)
    counts = jnp.where(heavy_pick == 0, SLOTS, base_counts)
    top_device = jax.random.randint(top_key, (), 0, N_FSDP)
    counts = jnp.where(jnp.arange(N_FSDP) == top_device, SLOTS, counts)
    return counts.astype(jnp.int32)


def with_ends(result, stream_key, least, largest):
    shape = result.shape
    spot = [jax.random.randint(jax.random.fold_in(stream_key, axis), (), 0, shape[axis]) for axis in range(len(shape))]
    result = result.at[tuple(spot)].set(least)
    longest = shape.index(max(shape))
    spot[longest] = (spot[longest] + 1) % shape[longest]
    return result.at[tuple(spot)].set(largest)


def level_of(key, extent, shards, low, top_value):
    loudness = 1.0
    for axis_at, shards_of in shards:
        heights = jax.random.uniform(jax.random.fold_in(jax.random.fold_in(key, 6), axis_at), (shards_of,), jnp.float32, low / len(shards), top_value / len(shards))
        loudness = loudness * jnp.repeat(jnp.exp(heights), extent[axis_at] // shards_of).reshape((-1,) + (1,) * (len(extent) - 1 - axis_at))
    return loudness


def noise(rng, extent, spread, limit, cuts=(), kind=jnp.bfloat16):
    gain = level_of(rng, extent, cuts, -0.22, 0.18) if cuts else 1.0
    array = jax.random.normal(rng, extent, jnp.float32) * spread * gain
    return jnp.minimum(jnp.maximum(array, -limit), limit).astype(kind)


def setup_inputs(seed: int = 0, part: int = 0) -> dict:
    streams_of = jax.random.split(jax.random.key(seed), 8)
    own_keys = jax.random.split(jax.random.fold_in(streams_of[7], part), 8)
    tokens = noise(own_keys[0], (TOKENS, D), 1.0, 6.0, ((0, 8), (1, 2)))
    cotangent = noise(own_keys[1], (TOKENS, DV), 0.01, 0.059814453, ((0, 8), (1, 2)))
    frozen_rows = noise(streams_of[2], (DV, D), D ** -0.5, 0.0625, ((0, 8), (1, 2)))
    rank_down = noise(own_keys[3], (TENANTS * RANK, D), D ** -0.5, 0.0625, ((0, 8), (1, 2)))
    rank_up = noise(own_keys[4], (TENANTS * RANK, DV), RANK ** -0.5, 1.5, ((0, 8), (1, 2)))
    counts = draw_counts(jax.random.fold_in(jax.random.fold_in(streams_of[7], part), 71), part)
    tenants = with_ends(jax.random.randint(own_keys[6], (N_FSDP * SLOTS,), 0, TENANTS), jax.random.fold_in(own_keys[6], 1), 0, TENANTS - 1).astype(jnp.int32)
    return {"tokens": tokens, "cotangent": cotangent, "frozen_rows": frozen_rows, "rank_down": rank_down, "rank_up": rank_up, "counts": counts, "tenants": tenants}


adapter_scale = 2.0


def reference(tokens, cotangent, frozen_rows, rank_down, rank_up, counts, tenants):
    blocks = N_FSDP * SLOTS
    token_blocks = tokens.reshape(blocks, BLOCK, D)
    cot_blocks = cotangent.reshape(blocks, BLOCK, DV)
    is_live = (jnp.arange(blocks, dtype=jnp.int32) % SLOTS) < jnp.repeat(counts, SLOTS)
    contract = (((1,), (1,)), ((), ()))
    columns = (((0,), (0,)), ((), ()))

    def advance(carried, element):
        grad_down, grad_up = carried
        row_block, cot_block, tenant, active_current = element
        offset = (tenant * RANK).astype(jnp.int32)
        down_rows = lax.dynamic_slice_in_dim(rank_down, offset, RANK, 0)
        up_weight_rows = lax.dynamic_slice_in_dim(rank_up, offset, RANK, 0)
        frozen_portion = lax.dot_general(row_block, frozen_rows, contract, preferred_element_type=jnp.float32)
        lower_half = lax.dot_general(row_block, down_rows, contract, preferred_element_type=jnp.float32).astype(jnp.bfloat16)
        back_half = lax.dot_general(cot_block, up_weight_rows, contract, preferred_element_type=jnp.float32).astype(jnp.bfloat16)
        final_result = (frozen_portion + adapter_scale * jnp.dot(lower_half, up_weight_rows, preferred_element_type=jnp.float32)).astype(jnp.bfloat16)
        final_result = jnp.where(active_current, final_result, jnp.zeros_like(final_result))
        scaling_factor = jnp.where(active_current, adapter_scale, 0.0).astype(jnp.float32)
        down_projection_term = scaling_factor * lax.dot_general(back_half, row_block, columns, preferred_element_type=jnp.float32)
        up_projection_term = scaling_factor * lax.dot_general(lower_half, cot_block, columns, preferred_element_type=jnp.float32)
        grad_down = lax.dynamic_update_slice_in_dim(grad_down, lax.dynamic_slice_in_dim(grad_down, offset, RANK, 0) + down_projection_term, offset, 0)
        grad_up = lax.dynamic_update_slice_in_dim(grad_up, lax.dynamic_slice_in_dim(grad_up, offset, RANK, 0) + up_projection_term, offset, 0)
        return (grad_down, grad_up), final_result

    start_grads = (jnp.zeros((TENANTS * RANK, D), jnp.float32), jnp.zeros((TENANTS * RANK, DV), jnp.float32))
    (grad_down, grad_up), results = lax.scan(advance, start_grads, (token_blocks, cot_blocks, tenants, is_live))
    return results.reshape(TOKENS, DV), grad_down, grad_up
```

```python
import jax
import jax.numpy as jnp
from jax import lax
from jax.sharding import PartitionSpec as P

RANK = 16
BLOCK = 512
SLOTS = 2
SCALE = 2.0

CONTRACT = (((1,), (1,)), ((), ()))
COLUMNS = (((0,), (0,)), ((), ()))


def gather(x):
    return lax.all_gather(x, "fsdp", axis=0, tiled=True)


def rows_of(table, tenants):
    return [
        lax.dynamic_slice_in_dim(table, tenants[s] * RANK, RANK, 0) for s in range(SLOTS)
    ]


def owner_sum(terms, chosen):
    return jnp.dot(chosen, terms, preferred_element_type=jnp.float32)


def swap_cores(x):
    return lax.ppermute(x, "tp", [(0, 1), (1, 0)])


def sum_cores(x):
    return x + swap_cores(x)


def local(tokens, cotangent, frozen_rows, rank_down, rank_up, counts, tenants):
    me = lax.axis_index("fsdp")
    owned = rank_down.shape[0]
    live = jnp.arange(SLOTS, dtype=jnp.int32) < counts[0]
    live_f = jnp.where(live, SCALE, 0.0).astype(jnp.float32)
    x = [tokens[s * BLOCK : (s + 1) * BLOCK] for s in range(SLOTS)]
    g = [cotangent[s * BLOCK : (s + 1) * BLOCK] for s in range(SLOTS)]

    up_all = gather(rank_up)
    ids_all = gather(jnp.where(live, tenants, -1))
    mine = me * owned + jnp.arange(owned, dtype=jnp.int32)
    sent = (ids_all[:, None] * RANK + jnp.arange(RANK, dtype=jnp.int32)).reshape(-1)
    chosen = (mine[:, None] == sent[None, :]).astype(jnp.bfloat16)

    up = rows_of(up_all, tenants)
    back_part = jnp.stack(
        [lax.dot_general(g[s], up[s], CONTRACT, preferred_element_type=jnp.float32) for s in range(SLOTS)]
    )
    back = sum_cores(back_part).astype(jnp.bfloat16)
    down_terms = jnp.concatenate(
        [
            (live_f[s] * lax.dot_general(back[s], x[s], COLUMNS, preferred_element_type=jnp.float32))
            for s in range(SLOTS)
        ]
    ).astype(jnp.bfloat16)
    down_all = gather(rank_down)
    down_terms_all = gather(down_terms)
    frozen_all = gather(frozen_rows)

    down = rows_of(down_all, tenants)
    low_part = jnp.stack(
        [lax.dot_general(x[s], down[s], CONTRACT, preferred_element_type=jnp.float32) for s in range(SLOTS)]
    )
    low = sum_cores(low_part).astype(jnp.bfloat16)
    up_terms = jnp.concatenate(
        [
            (live_f[s] * lax.dot_general(low[s], g[s], COLUMNS, preferred_element_type=jnp.float32))
            for s in range(SLOTS)
        ]
    ).astype(jnp.bfloat16)
    up_terms_all = gather(up_terms)
    grad_down = owner_sum(down_terms_all, chosen)
    grad_up = owner_sum(up_terms_all, chosen)

    half = cotangent.shape[1]
    core = lax.axis_index("tp")

    def frozen_half(which):
        weight = lax.dynamic_slice_in_dim(frozen_all, which * half, half, 0)
        return lax.dot_general(tokens, weight, CONTRACT, preferred_element_type=jnp.float32)

    received = swap_cores(frozen_half(1 - core))
    frozen = frozen_half(core) + received
    adapted = jnp.concatenate(
        [
            SCALE * jnp.dot(low[s], up[s], preferred_element_type=jnp.float32)
            for s in range(SLOTS)
        ]
    )
    keep = jnp.repeat(live, BLOCK)[:, None]
    projected = jnp.where(keep, frozen + adapted, 0.0).astype(jnp.bfloat16)
    return projected, grad_down, grad_up


def solution(mesh):
    rows = P(("group", "fsdp"), "tp")
    flat = P(("group", "fsdp"))
    in_specs = (rows, rows, P("fsdp", "tp"), rows, rows, flat, flat)
    return jax.shard_map(
        local, mesh=mesh, in_specs=in_specs, out_specs=(rows, rows, rows), check_vma=False
    )
```

```python
import functools

import jax
import jax.numpy as jnp
from jax import lax
from jax.experimental import pallas as pl
from jax.experimental.pallas import tpu as pltpu
from jax.sharding import PartitionSpec as P

RANK = 16
BLOCK = 512
SLOTS = 2
SCALE = 2.0

CONTRACT = (((1,), (1,)), ((), ()))
COLUMNS = (((0,), (0,)), ((), ()))


RING_LIMIT = 16
MESH = pl.DeviceIdType.MESH


def ring_kernel(n, plan, *refs):
    count = len(plan)
    ins, outs = refs[:count], refs[count : 2 * count]
    own_sem, send_sem, recv_sem, x_send, x_recv = refs[2 * count :]
    depth = n // 2
    group, me, core = lax.axis_index("group"), lax.axis_index("fsdp"), lax.axis_index("tp")

    def place(r):
        far = r // depth
        return 2 * (r + far * (2 * depth - 1 - 2 * r)) + far

    row = me // 2
    side = me % 2
    spot = row + side * (2 * depth - 1 - 2 * row)
    ways = (
        (group, place((spot + 1) % n), core),
        (group, place((spot + n - 1) % n), core),
    )
    across = (1 - group, me, core)
    shares = any(shared for _, shared in plan)

    barrier = pltpu.get_barrier_semaphore()
    greeted = ways + ((across,) if shares else ())
    for other in greeted:
        pl.semaphore_signal(barrier, inc=1, device_id=other, device_id_type=MESH)
    pl.semaphore_wait(barrier, len(greeted))

    def pieces(k):
        halves, shared = plan[k]
        rows = ins[k].shape[0]
        part = rows // 2 if shared else rows
        size = part // halves
        base = group * part if shared else 0
        return [(base + h * size, size) for h in range(halves)]

    copies, hand_overs = {}, []

    def send(k, h, d, step):
        low, size = pieces(k)[h]
        origin = place((spot + (n - step if d == 0 else step)) % n)
        there = pl.ds(pl.multiple_of(origin * ins[k].shape[0] + low, 8), size)
        here = ins[k].at[pl.ds(pl.multiple_of(low, 8), size)] if step == 0 else outs[k].at[there]
        at = k, h, d, step
        copy = pltpu.make_async_remote_copy(
            src_ref=here,
            dst_ref=outs[k].at[there],
            send_sem=send_sem.at[at],
            recv_sem=recv_sem.at[at],
            device_id=ways[d],
            device_id_type=MESH,
        )
        copy.start()
        copies[at] = copy

    def arrived(k, h, d, step):
        copies[k, h, d, step].wait_recv()
        if plan[k][1]:
            low, size = pieces(k)[h]
            step = step + 1
            origin = place((spot + (n - step if d == 0 else step)) % n)
            there = outs[k].at[pl.ds(pl.multiple_of(origin * ins[k].shape[0] + low, 8), size)]
            copy = pltpu.make_async_remote_copy(
                src_ref=there,
                dst_ref=there,
                send_sem=x_send.at[h, d, step - 1],
                recv_sem=x_recv.at[h, d, step - 1],
                device_id=across,
                device_id_type=MESH,
            )
            copy.start()
            hand_overs.append(copy)

    def hops(h, d):
        return depth if h == d else depth - 1

    own = []
    for step in range(depth + 1):
        for k in range(count):
            for h in range(plan[k][0]):
                for d in range(2):
                    if 1 <= step <= hops(h, d):
                        arrived(k, h, d, step - 1)
                    if step < hops(h, d):
                        send(k, h, d, step)
        if step == 0:
            for k in range(count):
                rows = ins[k].shape[0]
                copy = pltpu.make_async_copy(
                    ins[k], outs[k].at[pl.ds(pl.multiple_of(me * rows, 8), rows)], own_sem.at[k]
                )
                copy.start()
                own.append(copy)
    for copy in hand_overs:
        copy.wait_recv()
    for copy in list(copies.values()) + hand_overs:
        copy.wait_send()
    for copy in own:
        copy.wait()


def gather(arrays, plan, identity):
    n = lax.axis_size("fsdp")
    if n > RING_LIMIT or n % 2 or lax.axis_size("group") != 2:
        return [lax.all_gather(x, "fsdp", axis=0, tiled=True) for x in arrays]
    sems = (len(arrays), 2, 2, n // 2)
    whole = pl.BlockSpec(memory_space=pl.ANY)
    moved = sum(x.size * x.dtype.itemsize for x in arrays)
    return pl.pallas_call(
        functools.partial(ring_kernel, n, plan),
        out_shape=[jax.ShapeDtypeStruct((n * x.shape[0], x.shape[1]), x.dtype) for x in arrays],
        in_specs=[whole] * len(arrays),
        out_specs=[whole] * len(arrays),
        scratch_shapes=[
            pltpu.SemaphoreType.DMA((len(arrays),)),
            pltpu.SemaphoreType.DMA(sems),
            pltpu.SemaphoreType.DMA(sems),
            pltpu.SemaphoreType.DMA(sems[1:]),
            pltpu.SemaphoreType.DMA(sems[1:]),
        ],
        compiler_params=pltpu.CompilerParams(collective_id=identity, has_side_effects=True),
        cost_estimate=pl.CostEstimate(flops=0, bytes_accessed=2 * n * moved, transcendentals=0),
    )(*arrays)


def rows_of(table, tenants):
    return [
        lax.dynamic_slice_in_dim(table, tenants[s] * RANK, RANK, 0) for s in range(SLOTS)
    ]


def owner_sum(terms, chosen):
    return jnp.dot(chosen, terms, preferred_element_type=jnp.float32)


def swap_cores(x):
    return lax.ppermute(x, "tp", [(0, 1), (1, 0)])


def sum_cores(x):
    return x + swap_cores(x)


def local(tokens, cotangent, frozen_rows, rank_down, rank_up, counts, tenants):
    me = lax.axis_index("fsdp")
    owned = rank_down.shape[0]
    live = jnp.arange(SLOTS, dtype=jnp.int32) < counts[0]
    live_f = jnp.where(live, SCALE, 0.0).astype(jnp.float32)
    x = [tokens[s * BLOCK : (s + 1) * BLOCK] for s in range(SLOTS)]
    g = [cotangent[s * BLOCK : (s + 1) * BLOCK] for s in range(SLOTS)]

    ids = jnp.where(live, tenants, -1)
    ids_tile = jnp.broadcast_to(jnp.pad(ids, (0, 8 - SLOTS))[:, None], (8, 128))
    up_all, tiles_all = gather([rank_up, ids_tile], [(2, False), (1, False)], 0)
    ids_all = tiles_all[:, 0].reshape(-1, 8)[:, :SLOTS].reshape(-1)
    mine = me * owned + jnp.arange(owned, dtype=jnp.int32)
    sent = (ids_all[:, None] * RANK + jnp.arange(RANK, dtype=jnp.int32)).reshape(-1)
    chosen = (mine[:, None] == sent[None, :]).astype(jnp.bfloat16)

    up = rows_of(up_all, tenants)
    back_part = jnp.stack(
        [lax.dot_general(g[s], up[s], CONTRACT, preferred_element_type=jnp.float32) for s in range(SLOTS)]
    )
    back = sum_cores(back_part).astype(jnp.bfloat16)
    down_terms = jnp.concatenate(
        [
            (live_f[s] * lax.dot_general(back[s], x[s], COLUMNS, preferred_element_type=jnp.float32))
            for s in range(SLOTS)
        ]
    ).astype(jnp.bfloat16)
    frozen_all, down_all, down_terms_all = gather(
        [frozen_rows, rank_down, down_terms], [(2, True), (2, False), (2, False)], 1
    )

    down = rows_of(down_all, tenants)
    low_part = jnp.stack(
        [lax.dot_general(x[s], down[s], CONTRACT, preferred_element_type=jnp.float32) for s in range(SLOTS)]
    )
    low = sum_cores(low_part).astype(jnp.bfloat16)
    up_terms = jnp.concatenate(
        [
            (live_f[s] * lax.dot_general(low[s], g[s], COLUMNS, preferred_element_type=jnp.float32))
            for s in range(SLOTS)
        ]
    ).astype(jnp.bfloat16)
    (up_terms_all,) = gather([up_terms], [(2, False)], 2)
    grad_down = owner_sum(down_terms_all, chosen)
    grad_up = owner_sum(up_terms_all, chosen)

    half = cotangent.shape[1]
    core = lax.axis_index("tp")

    def frozen_half(which):
        weight = lax.dynamic_slice_in_dim(frozen_all, which * half, half, 0)
        return lax.dot_general(tokens, weight, CONTRACT, preferred_element_type=jnp.float32)

    received = swap_cores(frozen_half(1 - core))
    frozen = frozen_half(core) + received
    adapted = jnp.concatenate(
        [
            SCALE * jnp.dot(low[s], up[s], preferred_element_type=jnp.float32)
            for s in range(SLOTS)
        ]
    )
    keep = jnp.repeat(live, BLOCK)[:, None]
    projected = jnp.where(keep, frozen + adapted, 0.0).astype(jnp.bfloat16)
    return projected, grad_down, grad_up


def solution(mesh):
    rows = P(("group", "fsdp"), "tp")
    flat = P(("group", "fsdp"))
    in_specs = (rows, rows, P("fsdp", "tp"), rows, rows, flat, flat)
    return jax.shard_map(
        local, mesh=mesh, in_specs=in_specs, out_specs=(rows, rows, rows), check_vma=False
    )
```

```python
import functools

import jax
import jax.numpy as jnp
from jax import lax
from jax.experimental import pallas as pl
from jax.experimental.pallas import tpu as pltpu
from jax.sharding import PartitionSpec as P

RANK = 16
BLOCK = 512
SLOTS = 2
SCALE = 2.0

CONTRACT = (((1,), (1,)), ((), ()))
COLUMNS = (((0,), (0,)), ((), ()))


RING_LIMIT = 16
TILE = 256
MESH = pl.DeviceIdType.MESH


def ring_kernel(n, plan, fused, *refs):
    count = len(plan)
    ins, outs = refs[:count], refs[count : 2 * count]
    own_sem, send_sem, recv_sem, x_send, x_recv = refs[2 * count : 2 * count + 5]
    if fused:
        ins = refs[:count]
        tokens_ref, product_ref = refs[count], refs[count + 1]
        outs = refs[count + 2 : 2 * count + 1]
        (own_sem, send_sem, recv_sem, x_send, x_recv, gathered, held, part, other_part,
         load_sem, swap_send, swap_recv) = refs[2 * count + 1 :]
        outs = (gathered,) + tuple(outs)
    depth = n // 2
    group, me, core = lax.axis_index("group"), lax.axis_index("fsdp"), lax.axis_index("tp")

    def place(r):
        far = r // depth
        return 2 * (r + far * (2 * depth - 1 - 2 * r)) + far

    row = me // 2
    side = me % 2
    spot = row + side * (2 * depth - 1 - 2 * row)
    ways = (
        (group, place((spot + 1) % n), core),
        (group, place((spot + n - 1) % n), core),
    )
    across = (1 - group, me, core)
    twin = (group, me, 1 - core)
    shares = any(shared for _, shared in plan)

    barrier = pltpu.get_barrier_semaphore()
    greeted = ways + ((across,) if shares else ()) + ((twin,) if fused else ())
    for other in greeted:
        pl.semaphore_signal(barrier, inc=1, device_id=other, device_id_type=MESH)
    pl.semaphore_wait(barrier, len(greeted))

    def pieces(k):
        halves, shared = plan[k]
        rows = ins[k].shape[0]
        part = rows // 2 if shared else rows
        size = part // halves
        base = group * part if shared else 0
        return [(base + h * size, size) for h in range(halves)]

    copies, hand_overs = {}, []

    def send(k, h, d, step):
        low, size = pieces(k)[h]
        origin = place((spot + (n - step if d == 0 else step)) % n)
        there = pl.ds(pl.multiple_of(origin * ins[k].shape[0] + low, 8), size)
        here = ins[k].at[pl.ds(pl.multiple_of(low, 8), size)] if step == 0 else outs[k].at[there]
        at = k, h, d, step
        copy = pltpu.make_async_remote_copy(
            src_ref=here,
            dst_ref=outs[k].at[there],
            send_sem=send_sem.at[at],
            recv_sem=recv_sem.at[at],
            device_id=ways[d],
            device_id_type=MESH,
        )
        copy.start()
        copies[at] = copy

    def arrived(k, h, d, step):
        copies[k, h, d, step].wait_recv()
        if plan[k][1]:
            low, size = pieces(k)[h]
            step = step + 1
            origin = place((spot + (n - step if d == 0 else step)) % n)
            there = outs[k].at[pl.ds(pl.multiple_of(origin * ins[k].shape[0] + low, 8), size)]
            copy = pltpu.make_async_remote_copy(
                src_ref=there,
                dst_ref=there,
                send_sem=x_send.at[h, d, step - 1],
                recv_sem=x_recv.at[h, d, step - 1],
                device_id=across,
                device_id_type=MESH,
            )
            copy.start()
            hand_overs.append((step - 1, copy))

    def hops(h, d):
        return depth if h == d else depth - 1

    def swap(origin):
        return pltpu.make_async_remote_copy(
            src_ref=part.at[origin],
            dst_ref=other_part.at[origin % depth],
            send_sem=swap_send.at[origin % depth],
            recv_sem=swap_recv.at[origin % depth],
            device_id=twin,
            device_id_type=MESH,
        )

    def multiply(away):
        origin = place((spot + away + n) % n)
        rows = ins[0].shape[0]
        chunk = pl.ds(pl.multiple_of(origin * rows, 8), rows)

        def tile(t, carried):
            block = pl.ds(pl.multiple_of(t * TILE, TILE), TILE)
            part[origin, block] = lax.dot_general(
                held[block], gathered[chunk], CONTRACT, preferred_element_type=jnp.float32
            )
            return carried

        lax.fori_loop(0, held.shape[0] // TILE, tile, 0)

        @pl.when(origin // depth != core)
        def _():
            swap(origin).start()

    def use(distance):
        if not fused:
            return
        if distance == 0:
            loaded.wait()
            own[0].wait()
            multiply(0)
            return
        for copy in [c for at, c in hand_overs if at == distance - 1]:
            copy.wait_recv()
        multiply(distance)
        if distance < depth:
            multiply(-distance)

    own = []
    if fused:
        loaded = pltpu.make_async_copy(tokens_ref, held, load_sem)
    for step in range(depth + 1):
        if step >= 2:
            use(step - 2)
        if step == depth:
            use(step - 1)
        for k in range(count):
            for h in range(plan[k][0]):
                for d in range(2):
                    if 1 <= step <= hops(h, d):
                        arrived(k, h, d, step - 1)
                    if step < hops(h, d):
                        send(k, h, d, step)
        if step == 0:
            for k in range(count):
                rows = ins[k].shape[0]
                copy = pltpu.make_async_copy(
                    ins[k], outs[k].at[pl.ds(pl.multiple_of(me * rows, 8), rows)], own_sem.at[k]
                )
                copy.start()
                own.append(copy)
            if fused:
                loaded.start()
    if fused:
        use(depth)
        for j in range(depth):
            swap((1 - core) * depth + j).wait()
            rows = ins[0].shape[0]
            product_ref[:, j * rows : (j + 1) * rows] = part[core * depth + j] + other_part[j]
    else:
        for _, copy in hand_overs:
            copy.wait_recv()
    for copy in list(copies.values()) + [c for _, c in hand_overs]:
        copy.wait_send()
    for copy in own[1:] if fused else own:
        copy.wait()


def gather(arrays, plan, identity, tokens=None):
    n = lax.axis_size("fsdp")
    fused = tokens is not None
    if n > RING_LIMIT or n % 2 or lax.axis_size("group") != 2:
        full = [lax.all_gather(x, "fsdp", axis=0, tiled=True) for x in arrays]
        return [cores_product(tokens, full[0])] + full[1:] if fused else full
    sems = (len(arrays), 2, 2, n // 2)
    whole = pl.BlockSpec(memory_space=pl.ANY)
    moved = sum(x.size * x.dtype.itemsize for x in arrays)
    out_shape = [jax.ShapeDtypeStruct((n * x.shape[0], x.shape[1]), x.dtype) for x in arrays]
    out_specs = [whole] * len(arrays)
    operands = list(arrays)
    scratch = [
        pltpu.SemaphoreType.DMA((len(arrays),)),
        pltpu.SemaphoreType.DMA(sems),
        pltpu.SemaphoreType.DMA(sems),
        pltpu.SemaphoreType.DMA(sems[1:]),
        pltpu.SemaphoreType.DMA(sems[1:]),
    ]
    flops = 0
    limit = None
    if fused:
        tall, wide = tokens.shape
        rows = arrays[0].shape[0]
        operands.append(tokens)
        scratch += [
            pltpu.VMEM(out_shape[0].shape, arrays[0].dtype),
            pltpu.VMEM((tall, wide), tokens.dtype),
            pltpu.VMEM((n, tall, rows), jnp.float32),
            pltpu.VMEM((n // 2, tall, rows), jnp.float32),
            pltpu.SemaphoreType.DMA,
            pltpu.SemaphoreType.DMA((n // 2,)),
            pltpu.SemaphoreType.DMA((n // 2,)),
        ]
        out_shape[0] = jax.ShapeDtypeStruct((tall, n // 2 * rows), jnp.float32)
        out_specs[0] = pl.BlockSpec(memory_space=pltpu.VMEM)
        flops = 2 * tall * wide * n * rows
        limit = 40 * 1024 * 1024
    return pl.pallas_call(
        functools.partial(ring_kernel, n, plan, fused),
        out_shape=out_shape,
        in_specs=[whole] * len(operands),
        out_specs=out_specs,
        scratch_shapes=scratch,
        compiler_params=pltpu.CompilerParams(
            collective_id=identity, has_side_effects=True, vmem_limit_bytes=limit
        ),
        cost_estimate=pl.CostEstimate(flops=flops, bytes_accessed=2 * n * moved, transcendentals=0),
    )(*operands)


def cores_product(tokens, frozen_all):
    half = frozen_all.shape[0] // 2
    core = lax.axis_index("tp")

    def frozen_half(which):
        weight = lax.dynamic_slice_in_dim(frozen_all, which * half, half, 0)
        return lax.dot_general(tokens, weight, CONTRACT, preferred_element_type=jnp.float32)

    received = swap_cores(frozen_half(1 - core))
    return frozen_half(core) + received


def rows_of(table, tenants):
    return [
        lax.dynamic_slice_in_dim(table, tenants[s] * RANK, RANK, 0) for s in range(SLOTS)
    ]


def owner_sum(terms, chosen):
    return jnp.dot(chosen, terms, preferred_element_type=jnp.float32)


def swap_cores(x):
    return lax.ppermute(x, "tp", [(0, 1), (1, 0)])


def sum_cores(x):
    return x + swap_cores(x)


def local(tokens, cotangent, frozen_rows, rank_down, rank_up, counts, tenants):
    me = lax.axis_index("fsdp")
    owned = rank_down.shape[0]
    live = jnp.arange(SLOTS, dtype=jnp.int32) < counts[0]
    live_f = jnp.where(live, SCALE, 0.0).astype(jnp.float32)
    x = [tokens[s * BLOCK : (s + 1) * BLOCK] for s in range(SLOTS)]
    g = [cotangent[s * BLOCK : (s + 1) * BLOCK] for s in range(SLOTS)]

    ids = jnp.where(live, tenants, -1)
    ids_tile = jnp.broadcast_to(jnp.pad(ids, (0, 8 - SLOTS))[:, None], (8, 128))
    up_all, tiles_all, down_all = gather(
        [rank_up, ids_tile, rank_down], [(2, False), (1, False), (2, False)], 0
    )
    ids_all = tiles_all[:, 0].reshape(-1, 8)[:, :SLOTS].reshape(-1)
    mine = me * owned + jnp.arange(owned, dtype=jnp.int32)
    sent = (ids_all[:, None] * RANK + jnp.arange(RANK, dtype=jnp.int32)).reshape(-1)
    chosen = (mine[:, None] == sent[None, :]).astype(jnp.bfloat16)

    up = rows_of(up_all, tenants)
    back_part = jnp.stack(
        [lax.dot_general(g[s], up[s], CONTRACT, preferred_element_type=jnp.float32) for s in range(SLOTS)]
    )
    back = sum_cores(back_part).astype(jnp.bfloat16)
    down_terms = jnp.concatenate(
        [
            (live_f[s] * lax.dot_general(back[s], x[s], COLUMNS, preferred_element_type=jnp.float32))
            for s in range(SLOTS)
        ]
    ).astype(jnp.bfloat16)
    down = rows_of(down_all, tenants)
    low_part = jnp.stack(
        [lax.dot_general(x[s], down[s], CONTRACT, preferred_element_type=jnp.float32) for s in range(SLOTS)]
    )
    low = sum_cores(low_part).astype(jnp.bfloat16)
    up_terms = jnp.concatenate(
        [
            (live_f[s] * lax.dot_general(low[s], g[s], COLUMNS, preferred_element_type=jnp.float32))
            for s in range(SLOTS)
        ]
    ).astype(jnp.bfloat16)
    frozen, down_terms_all, up_terms_all = gather(
        [frozen_rows, down_terms, up_terms], [(2, True), (2, False), (2, False)], 1, tokens
    )
    grad_down = owner_sum(down_terms_all, chosen)
    grad_up = owner_sum(up_terms_all, chosen)

    adapted = jnp.concatenate(
        [
            SCALE * jnp.dot(low[s], up[s], preferred_element_type=jnp.float32)
            for s in range(SLOTS)
        ]
    )
    keep = jnp.repeat(live, BLOCK)[:, None]
    projected = jnp.where(keep, frozen + adapted, 0.0).astype(jnp.bfloat16)
    return projected, grad_down, grad_up


def solution(mesh):
    rows = P(("group", "fsdp"), "tp")
    flat = P(("group", "fsdp"))
    in_specs = (rows, rows, P("fsdp", "tp"), rows, rows, flat, flat)
    return jax.shard_map(
        local, mesh=mesh, in_specs=in_specs, out_specs=(rows, rows, rows), check_vma=False
    )
```

```python
import functools

import jax
import jax.numpy as jnp
from jax import lax
from jax.experimental import pallas as pl
from jax.experimental.pallas import tpu as pltpu
from jax.sharding import PartitionSpec as P

RANK = 16
BLOCK = 512
SLOTS = 2
SCALE = 2.0

CONTRACT = (((1,), (1,)), ((), ()))
COLUMNS = (((0,), (0,)), ((), ()))


RING_LIMIT = 16
TILE = 512
MESH = pl.DeviceIdType.MESH


def ring_kernel(n, plan, fused, *refs):
    count = len(plan)
    ins, outs = refs[:count], refs[count : 2 * count]
    own_sem, send_sem, recv_sem, x_send, x_recv = refs[2 * count : 2 * count + 5]
    if fused:
        ins = refs[:count]
        tokens_ref, early_ref, product_ref = refs[count : count + 3]
        outs = refs[count + 3 : 2 * count + 2]
        (own_sem, send_sem, recv_sem, x_send, x_recv, gathered, held, part, other_part,
         early, load_sem, swap_send, swap_recv) = refs[2 * count + 2 :]
        outs = (gathered,) + tuple(outs)
    depth = n // 2
    group, me, core = lax.axis_index("group"), lax.axis_index("fsdp"), lax.axis_index("tp")

    def place(r):
        far = r // depth
        return 2 * (r + far * (2 * depth - 1 - 2 * r)) + far

    row = me // 2
    side = me % 2
    spot = row + side * (2 * depth - 1 - 2 * row)
    ways = (
        (group, place((spot + 1) % n), core),
        (group, place((spot + n - 1) % n), core),
    )
    across = (1 - group, me, core)
    twin = (group, me, 1 - core)
    shares = any(shared for _, shared in plan)

    barrier = pltpu.get_barrier_semaphore()
    greeted = ways + ((across,) if shares else ()) + ((twin,) if fused else ())
    for other in greeted:
        pl.semaphore_signal(barrier, inc=1, device_id=other, device_id_type=MESH)
    pl.semaphore_wait(barrier, len(greeted))

    def pieces(k):
        halves, shared = plan[k]
        rows = ins[k].shape[0]
        part = rows // 2 if shared else rows
        size = part // halves
        base = group * part if shared else 0
        return [(base + h * size, size) for h in range(halves)]

    copies, hand_overs = {}, []

    def send(k, h, d, step):
        low, size = pieces(k)[h]
        origin = place((spot + (n - step if d == 0 else step)) % n)
        there = pl.ds(pl.multiple_of(origin * ins[k].shape[0] + low, 8), size)
        here = ins[k].at[pl.ds(pl.multiple_of(low, 8), size)] if step == 0 else outs[k].at[there]
        at = k, h, d, step
        copy = pltpu.make_async_remote_copy(
            src_ref=here,
            dst_ref=outs[k].at[there],
            send_sem=send_sem.at[at],
            recv_sem=recv_sem.at[at],
            device_id=ways[d],
            device_id_type=MESH,
        )
        copy.start()
        copies[at] = copy

    def arrived(k, h, d, step):
        copies[k, h, d, step].wait_recv()
        if plan[k][1]:
            low, size = pieces(k)[h]
            step = step + 1
            origin = place((spot + (n - step if d == 0 else step)) % n)
            there = outs[k].at[pl.ds(pl.multiple_of(origin * ins[k].shape[0] + low, 8), size)]
            copy = pltpu.make_async_remote_copy(
                src_ref=there,
                dst_ref=there,
                send_sem=x_send.at[h, d, step - 1],
                recv_sem=x_recv.at[h, d, step - 1],
                device_id=across,
                device_id_type=MESH,
            )
            copy.start()
            hand_overs.append((step - 1, copy))

    def hops(h, d):
        return depth if h == d else depth - 1

    def swap(origin):
        return pltpu.make_async_remote_copy(
            src_ref=part.at[origin],
            dst_ref=other_part.at[origin % depth],
            send_sem=swap_send.at[origin % depth],
            recv_sem=swap_recv.at[origin % depth],
            device_id=twin,
            device_id_type=MESH,
        )

    def multiply(*aways):
        origins = [place((spot + away + n) % n) for away in aways]
        late = ins[0].shape[0]
        first = early.shape[0] // n
        rows = first + late

        def tile(t, carried):
            block = pl.ds(pl.multiple_of(t * TILE, TILE), TILE)
            weight = jnp.concatenate(
                [
                    source[pl.ds(pl.multiple_of(origin * size, 8), size)]
                    for origin in origins
                    for source, size in ((early, first), (gathered, late))
                ]
            )
            product = lax.dot_general(
                held[block], weight, CONTRACT, preferred_element_type=jnp.float32
            )
            for i, origin in enumerate(origins):
                part[origin, block] = product[:, i * rows : (i + 1) * rows]
            return carried

        lax.fori_loop(0, held.shape[0] // TILE, tile, 0)

        for origin in origins:

            @pl.when(origin // depth != core)
            def _(origin=origin):
                swap(origin).start()

    def use(distance):
        if not fused:
            return
        if distance == 0:
            for copy in loaded:
                copy.wait()
            own[0].wait()
            multiply(0)
            return
        for copy in [c for at, c in hand_overs if at == distance - 1]:
            copy.wait_recv()
        multiply(*((distance, -distance) if distance < depth else (distance,)))

    own = []
    if fused:
        loaded = [
            pltpu.make_async_copy(tokens_ref, held, load_sem.at[0]),
            pltpu.make_async_copy(early_ref, early, load_sem.at[1]),
        ]
    for step in range(depth + 1):
        if step >= 2:
            use(step - 2)
        if step == depth:
            use(step - 1)
        for k in range(count):
            for h in range(plan[k][0]):
                for d in range(2):
                    if 1 <= step <= hops(h, d):
                        arrived(k, h, d, step - 1)
                    if step < hops(h, d):
                        send(k, h, d, step)
        if step == 0:
            for k in range(count):
                rows = ins[k].shape[0]
                copy = pltpu.make_async_copy(
                    ins[k], outs[k].at[pl.ds(pl.multiple_of(me * rows, 8), rows)], own_sem.at[k]
                )
                copy.start()
                own.append(copy)
            if fused:
                for copy in loaded:
                    copy.start()
    if fused:
        use(depth)
        for j in range(depth):
            swap((1 - core) * depth + j).wait()
            rows = part.shape[2]
            product_ref[:, j * rows : (j + 1) * rows] = part[core * depth + j] + other_part[j]
    else:
        for _, copy in hand_overs:
            copy.wait_recv()
    for copy in list(copies.values()) + [c for _, c in hand_overs]:
        copy.wait_send()
    for copy in own[1:] if fused else own:
        copy.wait()


def gather(arrays, plan, identity, tokens=None, early=None):
    n = lax.axis_size("fsdp")
    fused = tokens is not None
    if n > RING_LIMIT or n % 2 or lax.axis_size("group") != 2:
        full = [lax.all_gather(x, "fsdp", axis=0, tiled=True) for x in arrays]
        if fused:
            both = [x.reshape(n, -1, x.shape[1]) for x in (early, full[0])]
            joined = jnp.concatenate(both, axis=1).reshape(-1, early.shape[1])
            full[0] = cores_product(tokens, joined)
        return full
    sems = (len(arrays), 2, 2, n // 2)
    whole = pl.BlockSpec(memory_space=pl.ANY)
    moved = sum(x.size * x.dtype.itemsize for x in arrays)
    out_shape = [jax.ShapeDtypeStruct((n * x.shape[0], x.shape[1]), x.dtype) for x in arrays]
    out_specs = [whole] * len(arrays)
    operands = list(arrays)
    scratch = [
        pltpu.SemaphoreType.DMA((len(arrays),)),
        pltpu.SemaphoreType.DMA(sems),
        pltpu.SemaphoreType.DMA(sems),
        pltpu.SemaphoreType.DMA(sems[1:]),
        pltpu.SemaphoreType.DMA(sems[1:]),
    ]
    flops = 0
    limit = None
    if fused:
        tall, wide = tokens.shape
        rows = arrays[0].shape[0] + early.shape[0] // n
        operands += [tokens, early]
        scratch += [
            pltpu.VMEM(out_shape[0].shape, arrays[0].dtype),
            pltpu.VMEM((tall, wide), tokens.dtype),
            pltpu.VMEM((n, tall, rows), jnp.float32),
            pltpu.VMEM((n // 2, tall, rows), jnp.float32),
            pltpu.VMEM(early.shape, early.dtype),
            pltpu.SemaphoreType.DMA((2,)),
            pltpu.SemaphoreType.DMA((n // 2,)),
            pltpu.SemaphoreType.DMA((n // 2,)),
        ]
        out_shape[0] = jax.ShapeDtypeStruct((tall, n // 2 * rows), jnp.float32)
        out_specs[0] = pl.BlockSpec(memory_space=pltpu.VMEM)
        flops = 2 * tall * wide * n * rows
        limit = 40 * 1024 * 1024
    return pl.pallas_call(
        functools.partial(ring_kernel, n, plan, fused),
        out_shape=out_shape,
        in_specs=[whole] * len(operands),
        out_specs=out_specs,
        scratch_shapes=scratch,
        compiler_params=pltpu.CompilerParams(
            collective_id=identity, has_side_effects=True, vmem_limit_bytes=limit
        ),
        cost_estimate=pl.CostEstimate(flops=flops, bytes_accessed=2 * n * moved, transcendentals=0),
    )(*operands)


def cores_product(tokens, frozen_all):
    half = frozen_all.shape[0] // 2
    core = lax.axis_index("tp")

    def frozen_half(which):
        weight = lax.dynamic_slice_in_dim(frozen_all, which * half, half, 0)
        return lax.dot_general(tokens, weight, CONTRACT, preferred_element_type=jnp.float32)

    received = swap_cores(frozen_half(1 - core))
    return frozen_half(core) + received


def rows_of(table, tenants):
    return [
        lax.dynamic_slice_in_dim(table, tenants[s] * RANK, RANK, 0) for s in range(SLOTS)
    ]


def owner_sum(terms, chosen):
    return jnp.dot(chosen, terms, preferred_element_type=jnp.float32)


def swap_cores(x):
    return lax.ppermute(x, "tp", [(0, 1), (1, 0)])


def sum_cores(x):
    return x + swap_cores(x)


def local(tokens, cotangent, frozen_rows, rank_down, rank_up, counts, tenants):
    me = lax.axis_index("fsdp")
    owned = rank_down.shape[0]
    live = jnp.arange(SLOTS, dtype=jnp.int32) < counts[0]
    live_f = jnp.where(live, SCALE, 0.0).astype(jnp.float32)
    x = [tokens[s * BLOCK : (s + 1) * BLOCK] for s in range(SLOTS)]
    g = [cotangent[s * BLOCK : (s + 1) * BLOCK] for s in range(SLOTS)]

    ids = jnp.where(live, tenants, -1)
    ids_tile = jnp.broadcast_to(jnp.pad(ids, (0, 8 - SLOTS))[:, None], (8, 128))
    middle = frozen_rows.shape[0] // 2
    up_all, tiles_all, down_all, early = gather(
        [rank_up, ids_tile, rank_down, frozen_rows[:middle]],
        [(2, False), (1, False), (2, False), (2, True)],
        0,
    )
    ids_all = tiles_all[:, 0].reshape(-1, 8)[:, :SLOTS].reshape(-1)
    mine = me * owned + jnp.arange(owned, dtype=jnp.int32)
    sent = (ids_all[:, None] * RANK + jnp.arange(RANK, dtype=jnp.int32)).reshape(-1)
    chosen = (mine[:, None] == sent[None, :]).astype(jnp.bfloat16)

    up = rows_of(up_all, tenants)
    back_part = jnp.stack(
        [lax.dot_general(g[s], up[s], CONTRACT, preferred_element_type=jnp.float32) for s in range(SLOTS)]
    )
    back = sum_cores(back_part).astype(jnp.bfloat16)
    down_terms = jnp.concatenate(
        [
            (live_f[s] * lax.dot_general(back[s], x[s], COLUMNS, preferred_element_type=jnp.float32))
            for s in range(SLOTS)
        ]
    ).astype(jnp.bfloat16)
    down = rows_of(down_all, tenants)
    low_part = jnp.stack(
        [lax.dot_general(x[s], down[s], CONTRACT, preferred_element_type=jnp.float32) for s in range(SLOTS)]
    )
    low = sum_cores(low_part).astype(jnp.bfloat16)
    up_terms = jnp.concatenate(
        [
            (live_f[s] * lax.dot_general(low[s], g[s], COLUMNS, preferred_element_type=jnp.float32))
            for s in range(SLOTS)
        ]
    ).astype(jnp.bfloat16)
    frozen, down_terms_all, up_terms_all = gather(
        [frozen_rows[middle:], down_terms, up_terms],
        [(2, True), (2, False), (2, False)],
        1,
        tokens,
        early,
    )
    grad_down = owner_sum(down_terms_all, chosen)
    grad_up = owner_sum(up_terms_all, chosen)

    adapted = jnp.concatenate(
        [
            SCALE * jnp.dot(low[s], up[s], preferred_element_type=jnp.float32)
            for s in range(SLOTS)
        ]
    )
    keep = jnp.repeat(live, BLOCK)[:, None]
    projected = jnp.where(keep, frozen + adapted, 0.0).astype(jnp.bfloat16)
    return projected, grad_down, grad_up


def solution(mesh):
    rows = P(("group", "fsdp"), "tp")
    flat = P(("group", "fsdp"))
    in_specs = (rows, rows, P("fsdp", "tp"), rows, rows, flat, flat)
    return jax.shard_map(
        local, mesh=mesh, in_specs=in_specs, out_specs=(rows, rows, rows), check_vma=False
    )
```
